32 devices in a mesh: groups: 2 (over y), pole: 2 (over core), grow: 2 (over x), gcol: 4 (over z).
Axes of the slice: x: 2, y: 2, z: 4, core: 2. Of those that a mesh axis runs over, the one named last changes fastest.
Arguments:
- inverse_block: bfloat16 [8, 2, 1024, 1024], P(('groups', 'pole'), None, 'grow', 'gcol'), parts along dimension 0, may hold values from -0.125 to 0.125
- lower_panel: bfloat16 [8, 2, 1024, 512], P(('groups', 'pole'), None, 'grow', 'gcol'), parts along dimension 0, may hold values from -6 to 6
- tile_pattern: int32 [8, 8], P('groups'), parts along dimension 0, may hold values 0 or 1
- diag_inverse: float32 [8, 2, 4, 128, 128], P(('groups', 'pole'), None, 'gcol'), parts along dimension 0, may hold values from -6 to 6
- pole_weight: float32 [8, 2], P(('groups', 'pole')), parts along dimension 0, may hold values from -4 to 4
Outputs:
- density_panel: float32 [2048, 512], P(('groups', 'grow'), 'gcol'), parts along dimension 0
- density_diag: float32 [8, 128, 128], P(('groups', 'gcol')), parts along dimension 0
The draws below stay inside these ranges and needn't reach their ends.
There are 2 independent parts, one for each index of `groups`. The reference program is written for one: setup_inputs(seed, part) draws one part's arguments, and reference() takes and returns one part's arrays. A program takes and returns all parts, laid end to end along the dimension named above; each array names one. Nothing has to cross between parts.
All inputs are finite; a program needn't handle non-finite values.
Results may differ from the reference program's by a relative error of at most 0.0029.
Values may be sent and summed in bfloat16 or wider, within the bound.
A program may use at most 64 MiB of HBM per device.

```python
import jax
import jax.numpy as jnp
from jax import lax

TILE = 128
NT = 8
N = 1024
NSUP = 4
POLES = 4


def place_ends(entries, key, least, largest):
    extent = entries.shape
    index_at = [jax.random.randint(jax.random.fold_in(key, axis), (), 0, extent[axis]) for axis in range(len(extent))]
    entries = entries.at[tuple(index_at)].set(least)
    longest = extent.index(max(extent))
    index_at[longest] = (index_at[longest] + 1) % extent[longest]
    return entries.at[tuple(index_at)].set(largest)


def block_scale(key, dims, pieces, low, high):
    loudness = 1.0
    for dim, shards_of in pieces:
        steps = jax.random.uniform(jax.random.fold_in(jax.random.fold_in(key, 6), dim), (shards_of,), jnp.float32, low / len(pieces), high / len(pieces))
        loudness = loudness * jnp.repeat(jnp.exp(steps), dims[dim] // shards_of).reshape((-1,) + (1,) * (len(dims) - 1 - dim))
    return loudness


def noise(own_key, shape, spread, bound, cuts=(), held_as=jnp.bfloat16):
    result = jax.random.normal(own_key, shape, jnp.float32) * spread
    if len(cuts) > 0:
        result = block_scale(own_key, shape, cuts, -0.22, 0.18) * result
    return jnp.clip(result, min=-bound, max=bound).astype(held_as)


def setup_inputs(seed: int = 0, part: int = 0) -> dict:
    splits = jax.random.split(jax.random.key(seed), 6)
    part_keys = jax.random.split(jax.random.fold_in(splits[5], part), 6)
    return {
        "inverse_block": noise(part_keys[0], (POLES, 2, N, N), (2 * N) ** -0.5, 0.125, ((0, 2), (2, 2), (3, 4))),
        "lower_panel": noise(part_keys[1], (POLES, 2, N, NSUP * TILE), 0.5, 6.0, ((0, 2), (2, 2), (3, 4))),
        "tile_pattern": place_ends((jax.random.randint(part_keys[2], (NSUP, NT), 0, 2) < 1).astype(jnp.int32), jax.random.fold_in(part_keys[2], 1), 0, 1),
        "diag_inverse": noise(part_keys[3], (POLES, 2, NSUP, TILE, TILE), 1.0, 6.0, ((0, 2), (2, 4)), jnp.float32),
        "pole_weight": noise(part_keys[4], (POLES, 2), 1.0, 4.0, ((0, 2),), jnp.float32),
    }


def pair_dot(left, right):
    return jnp.dot(left, right, preferred_element_type=jnp.float32)


def block_quad(left, right):
    return jnp.einsum("nka,nkb->kab", left, right, precision=lax.Precision.HIGHEST)


def reference(inverse_block, lower_panel, tile_pattern, diag_inverse, pole_weight):
    tile_mask = jnp.repeat(jnp.repeat(tile_pattern.T, TILE, axis=0), TILE, axis=1).astype(jnp.bfloat16)
    masked = lower_panel * tile_mask
    panel_total = jnp.zeros((N, NSUP * TILE), jnp.float32)
    diag_total = jnp.zeros((NSUP, TILE, TILE), jnp.float32)
    for pole_index in range(POLES):
        g_re = inverse_block[pole_index, 0]
        g_im = inverse_block[pole_index, 1]
        l_re = masked[pole_index, 0]
        l_im = masked[pole_index, 1]
        x_re = pair_dot(g_im, l_im) - pair_dot(g_re, l_re)
        x_im = -(pair_dot(g_re, l_im) + pair_dot(g_im, l_re))
        r_re = lax.optimization_barrier(x_re.astype(jnp.bfloat16)).astype(jnp.float32).reshape(N, NSUP, TILE)
        r_im = lax.optimization_barrier(x_im.astype(jnp.bfloat16)).astype(jnp.float32).reshape(N, NSUP, TILE)
        m_re = l_re.astype(jnp.float32).reshape(N, NSUP, TILE)
        m_im = l_im.astype(jnp.float32).reshape(N, NSUP, TILE)
        q_re = block_quad(m_re, r_re) - block_quad(m_im, r_im)
        q_im = block_quad(m_re, r_im) + block_quad(m_im, r_re)
        d_re = diag_inverse[pole_index, 0] - q_re
        d_im = diag_inverse[pole_index, 1] - q_im
        w_re = pole_weight[pole_index, 0]
        w_im = pole_weight[pole_index, 1]
        panel_total = panel_total + (w_re * x_re - w_im * x_im)
        diag_total = diag_total + (w_re * d_re - w_im * d_im)
    return panel_total, diag_total
```

```python
import functools

import jax
import jax.numpy as jnp
from jax import lax
from jax.experimental import pallas as pl
from jax.experimental.pallas import tpu as pltpu
from jax.sharding import PartitionSpec as P

TILE = 128
MESH = pl.DeviceIdType.MESH


def kernel(
    row_count,
    chunk,
    pattern_ref,
    weight_ref,
    inverse_ref,
    lower_ref,
    diag_ref,
    panel_out,
    diag_out,
    panels,
    inverse_next,
    total,
    panel_send,
    panel_recv,
    final,
    final_recv,
    quad,
    quad_send,
    quad_recv,
    shares,
    m_send,
    m_recv,
    x_send,
    x_recv,
    g_send,
    g_recv,
    p_send,
    p_recv,
    c_send,
    c_recv,
    q_send,
    q_recv,
    s_send,
    s_recv,
):
    poles, _, rows, half = inverse_ref.shape
    chunks = rows // chunk
    row_tiles = rows // TILE
    row = lax.axis_index("grow")
    col = lax.axis_index("gcol")
    core = lax.axis_index("pole")
    high, low = col // 2, col % 2
    inner = jnp.where(row == high, 0, 1)

    def to_high(step):
        return {"gcol": lax.rem(high + step, row_count) * 2 + low}

    def to_row(step):
        return {"grow": lax.rem(row + step, row_count)}

    def send_m(pole, step):
        return pltpu.make_async_remote_copy(
            src_ref=panels.at[0, high, pole],
            dst_ref=panels.at[0, high, pole],
            send_sem=m_send.at[step - 1, pole],
            recv_sem=m_recv.at[step - 1, pole],
            device_id=to_high(step),
            device_id_type=MESH,
        )

    def send_x(pole, step, across):
        sup = lax.rem(high + row_count - step, row_count)
        return pltpu.make_async_remote_copy(
            src_ref=panels.at[0, sup, pole],
            dst_ref=panels.at[1, sup, pole],
            send_sem=x_send.at[across - 1, step, pole],
            recv_sem=x_recv.at[step, pole],
            device_id=to_row(across),
            device_id_type=MESH,
        )

    def send_g(index):
        cut = pl.ds(pl.multiple_of(index * chunk, chunk), chunk)
        return pltpu.make_async_remote_copy(
            src_ref=inverse_ref.at[:, :, cut, :],
            dst_ref=inverse_next.at[:, :, cut, :],
            send_sem=g_send.at[index],
            recv_sem=g_recv.at[index],
            device_id={"gcol": high * 2 + 1 - low},
            device_id_type=MESH,
        )

    def send_p(index, step):
        return pltpu.make_async_remote_copy(
            src_ref=panel_send.at[index, lax.rem(high + step, row_count)],
            dst_ref=panel_recv.at[index, step - 1],
            send_sem=p_send.at[index, step - 1],
            recv_sem=p_recv.at[index, step - 1],
            device_id=to_high(step),
            device_id_type=MESH,
        )

    def send_c(index):
        return pltpu.make_async_remote_copy(
            src_ref=final.at[index],
            dst_ref=final_recv.at[index],
            send_sem=c_send.at[index],
            recv_sem=c_recv.at[index],
            device_id={"pole": 1 - core},
            device_id_type=MESH,
        )

    def send_q(step):
        return pltpu.make_async_remote_copy(
            src_ref=quad_send.at[lax.rem(high + step, row_count)],
            dst_ref=quad_recv.at[step - 1],
            send_sem=q_send.at[step - 1],
            recv_sem=q_recv.at[step - 1],
            device_id=to_high(step),
            device_id_type=MESH,
        )

    others = [(across, flip) for across in range(row_count) for flip in range(2) if (across, flip) != (0, 0)]

    def send_s(which):
        across, flip = others[which]
        return pltpu.make_async_remote_copy(
            src_ref=shares.at[row, core],
            dst_ref=shares.at[row, core],
            send_sem=s_send.at[which],
            recv_sem=s_recv.at[which],
            device_id={"grow": lax.rem(row + across, row_count), "pole": lax.rem(core + flip, 2)},
            device_id_type=MESH,
        )

    barrier = pltpu.get_barrier_semaphore()
    peers = [{"gcol": high * 2 + 1 - low}]
    peers += [to_high(step) for step in range(1, row_count)]
    peers += [
        {"grow": lax.rem(row + across, row_count), "pole": lax.rem(core + flip, 2)} for across, flip in others
    ]
    for peer in peers:
        pl.semaphore_signal(barrier, inc=1, device_id=peer, device_id_type=MESH)

    for tile in range(row_tiles):
        present = pattern_ref[col, row * row_tiles + tile].astype(jnp.float32).astype(jnp.bfloat16)
        cut = slice(tile * TILE, (tile + 1) * TILE)
        for pole in range(poles):
            panels[0, high, pole, :, cut, :] = lower_ref[pole, :, cut, :] * present

    pl.semaphore_wait(barrier, len(peers))

    for pole in range(poles):
        for step in range(1, row_count):
            send_m(pole, step).start()

    @pl.when(row == high)
    def _():
        for pole in range(poles):
            for across in range(1, row_count):
                send_x(pole, 0, across).start()

    for index in range(chunks):
        send_g(index).start()

    quad[...] = jnp.zeros_like(quad)

    for pole in range(poles):
        for step in range(1, row_count):
            send_m(pole, step).wait_recv()

            @pl.when(row == high)
            def _():
                for across in range(1, row_count):
                    send_x(pole, step, across).start()

    @pl.when(row != high)
    def _():
        for pole in range(poles):
            for step in range(row_count):
                send_x(pole, step, 1).wait_recv()

    def finish(index):
        cut = pl.ds(pl.multiple_of(index * chunk, chunk), chunk)
        value = total[high, cut, :]
        for step in range(1, row_count):
            send_p(index, step).wait_recv()
            value = value + panel_recv[index, step - 1].astype(jnp.float32)
        final[index] = value
        send_c(index).start()

    own_rows = pl.ds(pl.multiple_of(low * half, half), half)
    next_rows = pl.ds(pl.multiple_of((1 - low) * half, half), half)

    def dot(left, right):
        return jnp.dot(left, right, preferred_element_type=jnp.float32)

    def work(index, carry):
        cut = pl.ds(pl.multiple_of(index * chunk, chunk), chunk)
        send_g(index).wait_recv()
        for sup in range(row_count):
            summed = None
            for pole in range(poles):
                m_own = jnp.concatenate(
                    [panels[inner, sup, pole, 0, own_rows, :], panels[inner, sup, pole, 1, own_rows, :]], axis=1
                )
                m_next = jnp.concatenate(
                    [panels[inner, sup, pole, 0, next_rows, :], panels[inner, sup, pole, 1, next_rows, :]], axis=1
                )
                by_re = dot(inverse_ref[pole, 0, cut, :], m_own) + dot(inverse_next[pole, 0, cut, :], m_next)
                by_im = dot(inverse_ref[pole, 1, cut, :], m_own) + dot(inverse_next[pole, 1, cut, :], m_next)
                solved_re = by_im[:, TILE:] - by_re[:, :TILE]
                solved_im = -(by_re[:, TILE:] + by_im[:, :TILE])
                w_re, w_im = weight_ref[pole, 0], weight_ref[pole, 1]
                scaled_re = w_re * solved_re - w_im * solved_im
                scaled_im = w_re * solved_im + w_im * solved_re
                summed = scaled_re if summed is None else summed + scaled_re
                stacked = jnp.concatenate([-scaled_re, scaled_im], axis=0)
                upper = stacked.astype(jnp.bfloat16)
                rest = (stacked - upper.astype(jnp.float32)).astype(jnp.bfloat16)
                m_rows = jnp.concatenate(
                    [panels[0, sup, pole, 0, cut, :], panels[0, sup, pole, 1, cut, :]], axis=0
                )
                quad[sup] += lax.dot_general(
                    m_rows,
                    jnp.concatenate([upper, rest], axis=1),
                    (((0,), (0,)), ((), ())),
                    preferred_element_type=jnp.float32,
                )
            total[sup, cut, :] = summed
            panel_send[index, sup] = summed.astype(jnp.bfloat16)
        for step in range(1, row_count):
            send_p(index, step).start()

        @pl.when(index >= 1)
        def _():
            finish(index - 1)

        return carry

    lax.fori_loop(0, chunks, work, 0)

    for sup in range(row_count):
        quad_send[sup] = quad[sup, :, :TILE] + quad[sup, :, TILE:]
    for step in range(1, row_count):
        send_q(step).start()
    once = jnp.where(row == 0, 1.0, 0.0)
    share = quad_send[high]
    for pole in range(poles):
        share = share + (once * weight_ref[pole, 0]) * diag_ref[pole, 0, 0]
        share = share - (once * weight_ref[pole, 1]) * diag_ref[pole, 1, 0]
    finish(chunks - 1)
    for step in range(1, row_count):
        send_q(step).wait_recv()
        share = share + quad_recv[step - 1]
    shares[row, core] = share
    for which in range(len(others)):
        send_s(which).start()
    for index in range(chunks):
        send_c(index).wait_recv()
        panel_out[index * chunk : (index + 1) * chunk, :] = final[index] + final_recv[index]
    for which in range(len(others)):
        send_s(which).wait_recv()
    value = shares[0, 0]
    for at in range(1, 2 * row_count):
        value = value + shares[at // 2, at % 2]
    diag_out[0] = value

    for pole in range(poles):
        for step in range(1, row_count):
            send_m(pole, step).wait_send()

    @pl.when(row == high)
    def _():
        for pole in range(poles):
            for step in range(row_count):
                for across in range(1, row_count):
                    send_x(pole, step, across).wait_send()

    for index in range(chunks):
        send_g(index).wait_send()
        send_c(index).wait_send()
        for step in range(1, row_count):
            send_p(index, step).wait_send()
    for step in range(1, row_count):
        send_q(step).wait_send()
    for which in range(len(others)):
        send_s(which).wait_send()


def shards(row_count, inverse_block, lower_panel, tile_pattern, diag_inverse, pole_weight):
    poles, _, rows, half = inverse_block.shape
    chunk = 128
    chunks = rows // chunk
    vmem = pl.BlockSpec(memory_space=pltpu.VMEM)
    smem = pl.BlockSpec(memory_space=pltpu.SMEM)
    dma = pltpu.SemaphoreType.DMA
    bf16, f32 = jnp.bfloat16, jnp.float32
    steps = row_count - 1
    flops = 2 * poles * rows * half * 2 * TILE * row_count * 5
    return pl.pallas_call(
        functools.partial(kernel, row_count, chunk),
        out_shape=(
            jax.ShapeDtypeStruct((rows, TILE), f32),
            jax.ShapeDtypeStruct((1, TILE, TILE), f32),
        ),
        in_specs=[smem, smem, vmem, vmem, vmem],
        out_specs=(vmem, vmem),
        scratch_shapes=[
            pltpu.VMEM((2, row_count, poles, 2, rows, TILE), bf16),
            pltpu.VMEM((poles, 2, rows, half), bf16),
            pltpu.VMEM((row_count, rows, TILE), f32),
            pltpu.VMEM((chunks, row_count, chunk, TILE), bf16),
            pltpu.VMEM((chunks, steps, chunk, TILE), bf16),
            pltpu.VMEM((chunks, chunk, TILE), f32),
            pltpu.VMEM((chunks, chunk, TILE), f32),
            pltpu.VMEM((row_count, TILE, 2 * TILE), f32),
            pltpu.VMEM((row_count, TILE, TILE), f32),
            pltpu.VMEM((steps, TILE, TILE), f32),
            pltpu.VMEM((row_count, 2, TILE, TILE), f32),
            dma((steps, poles)),
            dma((steps, poles)),
            dma((steps, row_count, poles)),
            dma((row_count, poles)),
            dma((chunks,)),
            dma((chunks,)),
            dma((chunks, steps)),
            dma((chunks, steps)),
            dma((chunks,)),
            dma((chunks,)),
            dma((steps,)),
            dma((steps,)),
            dma((2 * row_count - 1,)),
            dma((2 * row_count - 1,)),
        ],
        compiler_params=pltpu.CompilerParams(
            collective_id=0, has_side_effects=True, vmem_limit_bytes=40 * 1024 * 1024
        ),
        cost_estimate=pl.CostEstimate(flops=flops, bytes_accessed=4 * 1024 * 1024, transcendentals=0),
    )(tile_pattern, pole_weight, inverse_block, lower_panel, diag_inverse)


def solution(mesh):
    placed = (
        P(("groups", "pole"), None, "grow", "gcol"),
        P(("groups", "pole"), None, "grow", "gcol"),
        P("groups", None),
        P(("groups", "pole"), None, "gcol", None, None),
        P(("groups", "pole"), None),
    )
    return jax.shard_map(
        functools.partial(shards, mesh.shape["grow"]),
        mesh=mesh,
        in_specs=placed,
        out_specs=(P(("groups", "grow"), "gcol"), P(("groups", "gcol"), None, None)),
        check_vma=False,
    )
```

```python
import functools

import jax
import jax.numpy as jnp
from jax import lax
from jax.experimental import pallas as pl
from jax.experimental.pallas import tpu as pltpu
from jax.sharding import PartitionSpec as P

TILE = 128
MESH = pl.DeviceIdType.MESH


def kernel(
    row_count,
    chunk,
    pattern_hbm,
    weight_hbm,
    inverse_hbm,
    lower_hbm,
    diag_hbm,
    panel_out,
    diag_out,
    pattern_ref,
    weight_ref,
    inverse_ref,
    lower_ref,
    diag_ref,
    load_sem,
    early,
    panels,
    inverse_next,
    total,
    panel_send,
    panel_recv,
    final,
    final_recv,
    quad,
    quad_send,
    quad_recv,
    shares,
    m_send,
    m_recv,
    x_send,
    x_recv,
    g_send,
    g_recv,
    p_send,
    p_recv,
    c_send,
    c_recv,
    q_send,
    q_recv,
    s_send,
    s_recv,
):
    poles, _, rows, half = inverse_ref.shape
    chunks = rows // chunk
    row_tiles = rows // TILE
    row = lax.axis_index("grow")
    col = lax.axis_index("gcol")
    core = lax.axis_index("pole")
    high, low = col // 2, col % 2
    inner = jnp.where(row == high, 0, 1)

    def to_high(step):
        return {"gcol": lax.rem(high + step, row_count) * 2 + low}

    def to_row(step):
        return {"grow": lax.rem(row + step, row_count)}

    def piece(at):
        return at // 2, pl.ds((at % 2) * (rows // 2), rows // 2)

    pieces = 2 * poles

    def send_m(at, step):
        pole, part = piece(at)
        return pltpu.make_async_remote_copy(
            src_ref=panels.at[0, high, pole, :, part],
            dst_ref=panels.at[0, high, pole, :, part],
            send_sem=m_send.at[step - 1, at],
            recv_sem=m_recv.at[step - 1, at],
            device_id=to_high(step),
            device_id_type=MESH,
        )

    def send_x(at, step, across):
        pole, part = piece(at)
        sup = lax.rem(high + row_count - step, row_count)
        return pltpu.make_async_remote_copy(
            src_ref=panels.at[0, sup, pole, :, part],
            dst_ref=panels.at[1, sup, pole, :, part],
            send_sem=x_send.at[across - 1, step, at],
            recv_sem=x_recv.at[step, at],
            device_id=to_row(across),
            device_id_type=MESH,
        )

    def send_g(index):
        cut = pl.ds(pl.multiple_of(index * chunk, chunk), chunk)
        return pltpu.make_async_remote_copy(
            src_ref=inverse_hbm.at[:, :, cut, :],
            dst_ref=inverse_next.at[:, :, cut, :],
            send_sem=g_send.at[index],
            recv_sem=g_recv.at[index],
            device_id={"gcol": high * 2 + 1 - low},
            device_id_type=MESH,
        )

    def send_p(index, step):
        return pltpu.make_async_remote_copy(
            src_ref=panel_send.at[index, lax.rem(high + step, row_count)],
            dst_ref=panel_recv.at[index, step - 1],
            send_sem=p_send.at[index, step - 1],
            recv_sem=p_recv.at[index, step - 1],
            device_id=to_high(step),
            device_id_type=MESH,
        )

    def send_c(index):
        return pltpu.make_async_remote_copy(
            src_ref=final.at[index],
            dst_ref=final_recv.at[index],
            send_sem=c_send.at[index],
            recv_sem=c_recv.at[index],
            device_id={"pole": 1 - core},
            device_id_type=MESH,
        )

    def send_q(step):
        return pltpu.make_async_remote_copy(
            src_ref=quad_send.at[lax.rem(high + step, row_count)],
            dst_ref=quad_recv.at[step - 1],
            send_sem=q_send.at[step - 1],
            recv_sem=q_recv.at[step - 1],
            device_id=to_high(step),
            device_id_type=MESH,
        )

    others = [(across, flip) for across in range(row_count) for flip in range(2) if (across, flip) != (0, 0)]

    def send_s(which):
        across, flip = others[which]
        return pltpu.make_async_remote_copy(
            src_ref=shares.at[row, core],
            dst_ref=shares.at[row, core],
            send_sem=s_send.at[which],
            recv_sem=s_recv.at[which],
            device_id={"grow": lax.rem(row + across, row_count), "pole": lax.rem(core + flip, 2)},
            device_id_type=MESH,
        )

    barrier = pltpu.get_barrier_semaphore()
    peers = [{"gcol": high * 2 + 1 - low}]
    peers += [to_high(step) for step in range(1, row_count)]
    peers += [
        {"grow": lax.rem(row + across, row_count), "pole": lax.rem(core + flip, 2)} for across, flip in others
    ]
    for peer in peers:
        pl.semaphore_signal(barrier, inc=1, device_id=peer, device_id_type=MESH)

    loads = [
        pltpu.make_async_copy(source, target, load_sem.at[at])
        for at, (source, target) in enumerate(
            (
                (pattern_hbm, pattern_ref),
                (lower_hbm, lower_ref),
                (weight_hbm, weight_ref),
                (inverse_hbm, inverse_ref),
                (diag_hbm, diag_ref),
            )
        )
    ]
    for load in loads:
        load.start()
    loads[0].wait()
    loads[1].wait()

    for tile in range(row_tiles):
        present = pattern_ref[col, row * row_tiles + tile].astype(jnp.float32).astype(jnp.bfloat16)
        cut = slice(tile * TILE, (tile + 1) * TILE)
        for pole in range(poles):
            panels[0, high, pole, :, cut, :] = lower_ref[pole, :, cut, :] * present

    pl.semaphore_wait(barrier, len(peers))

    for at in range(pieces):
        for step in range(1, row_count):
            send_m(at, step).start()

    @pl.when(row == high)
    def _():
        for at in range(pieces):
            for across in range(1, row_count):
                send_x(at, 0, across).start()

    ahead = 1
    for index in range(ahead):
        send_g(index).start()

    quad[...] = jnp.zeros_like(quad)
    for load in loads[2:]:
        load.wait()

    for at in range(pieces):
        for step in range(1, row_count):
            send_m(at, step).wait_recv()
            if step == 1:
                for index in ((), (1,), (), ())[at]:
                    send_g(index).start()

            @pl.when(row == high)
            def _():
                for across in range(1, row_count):
                    send_x(at, step, across).start()

    @pl.when(row != high)
    def _():
        for at in range(pieces):
            for step in range(row_count):
                send_x(at, step, 1).wait_recv()

    def finish(index):
        cut = pl.ds(pl.multiple_of(index * chunk, chunk), chunk)
        value = total[high, cut, :]
        for step in range(1, row_count):
            send_p(index, step).wait_recv()
            value = value + panel_recv[index, step - 1].astype(jnp.float32)
        final[index] = value
        send_c(index).start()

    own_rows = pl.ds(pl.multiple_of(low * half, half), half)
    next_rows = pl.ds(pl.multiple_of((1 - low) * half, half), half)

    def dot(left, right):
        return jnp.dot(left, right, preferred_element_type=jnp.float32)

    def begin(index, carry):
        cut = pl.ds(pl.multiple_of(index * chunk, chunk), chunk)
        for sup in range(row_count):
            for pole in range(poles):
                m_own = jnp.concatenate(
                    [panels[inner, sup, pole, 0, own_rows, :], panels[inner, sup, pole, 1, own_rows, :]], axis=1
                )
                for part in range(2):
                    early[pole, sup, part, cut, :] = dot(inverse_ref[pole, part, cut, :], m_own)
        return carry

    lax.fori_loop(0, chunks, begin, 0)

    def work(index, carry):
        cut = pl.ds(pl.multiple_of(index * chunk, chunk), chunk)
        send_g(index).wait_recv()
        for sup in range(row_count):
            summed = None
            for pole in range(poles):
                m_next = jnp.concatenate(
                    [panels[inner, sup, pole, 0, next_rows, :], panels[inner, sup, pole, 1, next_rows, :]], axis=1
                )
                by_re = early[pole, sup, 0, cut, :] + dot(inverse_next[pole, 0, cut, :], m_next)
                by_im = early[pole, sup, 1, cut, :] + dot(inverse_next[pole, 1, cut, :], m_next)
                solved_re = by_im[:, TILE:] - by_re[:, :TILE]
                solved_im = -(by_re[:, TILE:] + by_im[:, :TILE])
                w_re, w_im = weight_ref[pole, 0], weight_ref[pole, 1]
                scaled_re = w_re * solved_re - w_im * solved_im
                scaled_im = w_re * solved_im + w_im * solved_re
                summed = scaled_re if summed is None else summed + scaled_re
                stacked = jnp.concatenate([-scaled_re, scaled_im], axis=0)
                upper = stacked.astype(jnp.bfloat16)
                rest = (stacked - upper.astype(jnp.float32)).astype(jnp.bfloat16)
                m_rows = jnp.concatenate(
                    [panels[0, sup, pole, 0, cut, :], panels[0, sup, pole, 1, cut, :]], axis=0
                )
                quad[sup] += lax.dot_general(
                    m_rows,
                    jnp.concatenate([upper, rest], axis=1),
                    (((0,), (0,)), ((), ())),
                    preferred_element_type=jnp.float32,
                )
            total[sup, cut, :] = summed
            panel_send[index, sup] = summed.astype(jnp.bfloat16)

        @pl.when(index < chunks - 1)
        def _():
            for step in range(1, row_count):
                send_p(index, step).start()

        @pl.when(index >= 1)
        def _():
            finish(index - 1)

        return carry

    lax.fori_loop(0, chunks, work, 0)

    for sup in range(row_count):
        quad_send[sup] = (quad[sup, :, :TILE] + quad[sup, :, TILE:]).astype(jnp.bfloat16)
    for step in range(1, row_count):
        send_q(step).start()
    for step in range(1, row_count):
        send_p(chunks - 1, step).start()
    once = jnp.where(row == 0, 1.0, 0.0)
    share = quad[high, :, :TILE] + quad[high, :, TILE:]
    for pole in range(poles):
        share = share + (once * weight_ref[pole, 0]) * diag_ref[pole, 0, 0]
        share = share - (once * weight_ref[pole, 1]) * diag_ref[pole, 1, 0]
    finish(chunks - 1)
    for step in range(1, row_count):
        send_q(step).wait_recv()
        share = share + quad_recv[step - 1].astype(jnp.float32)
    shares[row, core] = share
    for which in range(len(others)):
        send_s(which).start()
    for index in range(chunks):
        send_c(index).wait_recv()
        panel_out[index * chunk : (index + 1) * chunk, :] = final[index] + final_recv[index]
    for which in range(len(others)):
        send_s(which).wait_recv()
    value = shares[0, 0]
    for at in range(1, 2 * row_count):
        value = value + shares[at // 2, at % 2]
    diag_out[0] = value

    for at in range(pieces):
        for step in range(1, row_count):
            send_m(at, step).wait_send()

    @pl.when(row == high)
    def _():
        for at in range(pieces):
            for step in range(row_count):
                for across in range(1, row_count):
                    send_x(at, step, across).wait_send()

    for index in range(chunks):
        send_g(index).wait_send()
        send_c(index).wait_send()
        for step in range(1, row_count):
            send_p(index, step).wait_send()
    for step in range(1, row_count):
        send_q(step).wait_send()
    for which in range(len(others)):
        send_s(which).wait_send()


def shards(row_count, inverse_block, lower_panel, tile_pattern, diag_inverse, pole_weight):
    poles, _, rows, half = inverse_block.shape
    chunk = 256
    chunks = rows // chunk
    vmem = pl.BlockSpec(memory_space=pltpu.VMEM)
    hbm = pl.BlockSpec(memory_space=pltpu.HBM)
    dma = pltpu.SemaphoreType.DMA
    bf16, f32 = jnp.bfloat16, jnp.float32
    steps = row_count - 1
    flops = 2 * poles * rows * half * 2 * TILE * row_count * 5
    return pl.pallas_call(
        functools.partial(kernel, row_count, chunk),
        out_shape=(
            jax.ShapeDtypeStruct((rows, TILE), f32),
            jax.ShapeDtypeStruct((1, TILE, TILE), f32),
        ),
        in_specs=[hbm] * 5,
        out_specs=(vmem, vmem),
        scratch_shapes=[
            pltpu.SMEM(tile_pattern.shape, jnp.int32),
            pltpu.SMEM(pole_weight.shape, f32),
            pltpu.VMEM(inverse_block.shape, bf16),
            pltpu.VMEM(lower_panel.shape, bf16),
            pltpu.VMEM(diag_inverse.shape, f32),
            dma((5,)),
            pltpu.VMEM((poles, row_count, 2, rows, 2 * TILE), f32),
            pltpu.VMEM((2, row_count, poles, 2, rows, TILE), bf16),
            pltpu.VMEM((poles, 2, rows, half), bf16),
            pltpu.VMEM((row_count, rows, TILE), f32),
            pltpu.VMEM((chunks, row_count, chunk, TILE), bf16),
            pltpu.VMEM((chunks, steps, chunk, TILE), bf16),
            pltpu.VMEM((chunks, chunk, TILE), f32),
            pltpu.VMEM((chunks, chunk, TILE), f32),
            pltpu.VMEM((row_count, TILE, 2 * TILE), f32),
            pltpu.VMEM((row_count, TILE, TILE), bf16),
            pltpu.VMEM((steps, TILE, TILE), bf16),
            pltpu.VMEM((row_count, 2, TILE, TILE), f32),
            dma((steps, 2 * poles)),
            dma((steps, 2 * poles)),
            dma((steps, row_count, 2 * poles)),
            dma((row_count, 2 * poles)),
            dma((chunks,)),
            dma((chunks,)),
            dma((chunks, steps)),
            dma((chunks, steps)),
            dma((chunks,)),
            dma((chunks,)),
            dma((steps,)),
            dma((steps,)),
            dma((2 * row_count - 1,)),
            dma((2 * row_count - 1,)),
        ],
        compiler_params=pltpu.CompilerParams(
            collective_id=0, has_side_effects=True, vmem_limit_bytes=62 * 1024 * 1024
        ),
        cost_estimate=pl.CostEstimate(flops=flops, bytes_accessed=4 * 1024 * 1024, transcendentals=0),
    )(tile_pattern, pole_weight, inverse_block, lower_panel, diag_inverse)


def solution(mesh):
    placed = (
        P(("groups", "pole"), None, "grow", "gcol"),
        P(("groups", "pole"), None, "grow", "gcol"),
        P("groups", None),
        P(("groups", "pole"), None, "gcol", None, None),
        P(("groups", "pole"), None),
    )
    return jax.shard_map(
        functools.partial(shards, mesh.shape["grow"]),
        mesh=mesh,
        in_specs=placed,
        out_specs=(P(("groups", "grow"), "gcol"), P(("groups", "gcol"), None, None)),
        check_vma=False,
    )
```

```python
import functools

import jax
import jax.numpy as jnp
from jax import lax
from jax.experimental import pallas as pl
from jax.experimental.pallas import tpu as pltpu
from jax.sharding import PartitionSpec as P

TILE = 128
MESH = pl.DeviceIdType.MESH


def kernel(
    row_count,
    chunk,
    pattern_hbm,
    weight_hbm,
    inverse_hbm,
    lower_hbm,
    diag_hbm,
    panel_out,
    diag_out,
    pattern_ref,
    weight_ref,
    inverse_ref,
    lower_ref,
    diag_ref,
    load_sem,
    early,
    panels,
    inverse_next,
    total,
    panel_send,
    panel_recv,
    final,
    final_recv,
    quad,
    quad_send,
    quad_recv,
    shares,
    m_send,
    m_recv,
    x_send,
    x_recv,
    g_send,
    g_recv,
    p_send,
    p_recv,
    c_send,
    c_recv,
    q_send,
    q_recv,
    s_send,
    s_recv,
):
    poles, _, rows, half = inverse_ref.shape
    chunks = rows // chunk
    row_tiles = rows // TILE
    row = lax.axis_index("grow")
    col = lax.axis_index("gcol")
    core = lax.axis_index("pole")
    high, low = col // 2, col % 2
    inner = jnp.where(row == high, 0, 1)

    def to_high(step):
        return {"gcol": lax.rem(high + step, row_count) * 2 + low}

    def to_row(step):
        return {"grow": lax.rem(row + step, row_count)}

    def piece(at):
        return at // 2, pl.ds((at % 2) * (rows // 2), rows // 2)

    pieces = 2 * poles

    def send_m(at, step):
        pole, part = piece(at)
        return pltpu.make_async_remote_copy(
            src_ref=panels.at[0, high, pole, :, part],
            dst_ref=panels.at[0, high, pole, :, part],
            send_sem=m_send.at[step - 1, at],
            recv_sem=m_recv.at[step - 1, at],
            device_id=to_high(step),
            device_id_type=MESH,
        )

    def send_x(at, step, across):
        pole, part = piece(at)
        sup = lax.rem(high + row_count - step, row_count)
        return pltpu.make_async_remote_copy(
            src_ref=panels.at[0, sup, pole, :, part],
            dst_ref=panels.at[1, sup, pole, :, part],
            send_sem=x_send.at[across - 1, step, at],
            recv_sem=x_recv.at[step, at],
            device_id=to_row(across),
            device_id_type=MESH,
        )

    def send_g(index):
        cut = pl.ds(pl.multiple_of(index * chunk, chunk), chunk)
        return pltpu.make_async_remote_copy(
            src_ref=inverse_hbm.at[:, :, cut, :],
            dst_ref=inverse_next.at[:, :, cut, :],
            send_sem=g_send.at[index],
            recv_sem=g_recv.at[index],
            device_id={"gcol": high * 2 + 1 - low},
            device_id_type=MESH,
        )

    def send_p(index, step):
        return pltpu.make_async_remote_copy(
            src_ref=panel_send.at[index, lax.rem(high + step, row_count)],
            dst_ref=panel_recv.at[index, step - 1],
            send_sem=p_send.at[index, step - 1],
            recv_sem=p_recv.at[index, step - 1],
            device_id=to_high(step),
            device_id_type=MESH,
        )

    def send_c(index):
        return pltpu.make_async_remote_copy(
            src_ref=final.at[index],
            dst_ref=final_recv.at[index],
            send_sem=c_send.at[index],
            recv_sem=c_recv.at[index],
            device_id={"pole": 1 - core},
            device_id_type=MESH,
        )

    def send_q(step):
        return pltpu.make_async_remote_copy(
            src_ref=quad_send.at[lax.rem(high + step, row_count)],
            dst_ref=quad_recv.at[step - 1],
            send_sem=q_send.at[step - 1],
            recv_sem=q_recv.at[step - 1],
            device_id=to_high(step),
            device_id_type=MESH,
        )

    others = [(across, flip) for across in range(row_count) for flip in range(2) if (across, flip) != (0, 0)]

    def send_s(which):
        across, flip = others[which]
        return pltpu.make_async_remote_copy(
            src_ref=shares.at[row, core],
            dst_ref=shares.at[row, core],
            send_sem=s_send.at[which],
            recv_sem=s_recv.at[which],
            device_id={"grow": lax.rem(row + across, row_count), "pole": lax.rem(core + flip, 2)},
            device_id_type=MESH,
        )

    barrier = pltpu.get_barrier_semaphore()
    peers = [{"gcol": high * 2 + 1 - low}]
    peers += [to_high(step) for step in range(1, row_count)]
    peers += [
        {"grow": lax.rem(row + across, row_count), "pole": lax.rem(core + flip, 2)} for across, flip in others
    ]
    for peer in peers:
        pl.semaphore_signal(barrier, inc=1, device_id=peer, device_id_type=MESH)

    loads = [
        pltpu.make_async_copy(source, target, load_sem.at[at])
        for at, (source, target) in enumerate(
            (
                (pattern_hbm, pattern_ref),
                (lower_hbm, lower_ref),
                (weight_hbm, weight_ref),
                (inverse_hbm, inverse_ref),
                (diag_hbm, diag_ref),
            )
        )
    ]
    for load in loads:
        load.start()
    loads[0].wait()
    loads[1].wait()

    for tile in range(row_tiles):
        present = pattern_ref[col, row * row_tiles + tile].astype(jnp.float32).astype(jnp.bfloat16)
        cut = slice(tile * TILE, (tile + 1) * TILE)
        for pole in range(poles):
            panels[0, high, pole, :, cut, :] = lower_ref[pole, :, cut, :] * present

    pl.semaphore_wait(barrier, len(peers))

    for at in range(pieces):
        for step in range(1, row_count):
            send_m(at, step).start()

    @pl.when(row == high)
    def _():
        for at in range(pieces):
            for across in range(1, row_count):
                send_x(at, 0, across).start()

    ahead = 1
    for index in range(ahead):
        send_g(index).start()

    quad[...] = jnp.zeros_like(quad)
    for load in loads[2:]:
        load.wait()

    for at in range(pieces):
        for step in range(1, row_count):
            send_m(at, step).wait_recv()
            if step == 1:
                for index in ((), (1,), (), ())[at]:
                    send_g(index).start()

            @pl.when(row == high)
            def _():
                for across in range(1, row_count):
                    send_x(at, step, across).start()

    @pl.when(row != high)
    def _():
        for at in range(pieces):
            for step in range(row_count):
                send_x(at, step, 1).wait_recv()

    def finish(index):
        cut = pl.ds(pl.multiple_of(index * chunk, chunk), chunk)
        value = total[high, cut, :]
        for step in range(1, row_count):
            send_p(index, step).wait_recv()
            value = value + panel_recv[index, step - 1].astype(jnp.float32)
        final[index] = value
        send_c(index).start()

    own_rows = pl.ds(pl.multiple_of(low * half, half), half)
    next_rows = pl.ds(pl.multiple_of((1 - low) * half, half), half)

    def dot(left, right):
        return jnp.dot(left, right, preferred_element_type=jnp.float32)

    def begin(index, carry):
        cut = pl.ds(pl.multiple_of(index * chunk, chunk), chunk)
        for sup in range(row_count):
            for pole in range(poles):
                m_own = jnp.concatenate(
                    [panels[inner, sup, pole, 0, own_rows, :], panels[inner, sup, pole, 1, own_rows, :]], axis=1
                )
                for part in range(2):
                    early[pole, sup, part, cut, :] = dot(inverse_ref[pole, part, cut, :], m_own)
        return carry

    lax.fori_loop(0, chunks, begin, 0)

    def work(index, carry):
        cut = pl.ds(pl.multiple_of(index * chunk, chunk), chunk)
        send_g(index).wait_recv()
        for sup in range(row_count):
            summed = None
            for pole in range(poles):
                m_next = jnp.concatenate(
                    [panels[inner, sup, pole, 0, next_rows, :], panels[inner, sup, pole, 1, next_rows, :]], axis=1
                )
                by_re = early[pole, sup, 0, cut, :] + dot(inverse_next[pole, 0, cut, :], m_next)
                by_im = early[pole, sup, 1, cut, :] + dot(inverse_next[pole, 1, cut, :], m_next)
                solved_re = by_im[:, TILE:] - by_re[:, :TILE]
                solved_im = -(by_re[:, TILE:] + by_im[:, :TILE])
                w_re, w_im = weight_ref[pole, 0], weight_ref[pole, 1]
                scaled_re = w_re * solved_re - w_im * solved_im
                scaled_im = w_re * solved_im + w_im * solved_re
                summed = scaled_re if summed is None else summed + scaled_re
                stacked = jnp.concatenate([-scaled_re, scaled_im], axis=0)
                upper = stacked.astype(jnp.bfloat16)
                rest = (stacked - upper.astype(jnp.float32)).astype(jnp.bfloat16)
                m_rows = jnp.concatenate(
                    [panels[0, sup, pole, 0, cut, :], panels[0, sup, pole, 1, cut, :]], axis=0
                )
                quad[sup] += lax.dot_general(
                    m_rows,
                    jnp.concatenate([upper, rest], axis=1),
                    (((0,), (0,)), ((), ())),
                    preferred_element_type=jnp.float32,
                )
            total[sup, cut, :] = summed
            panel_send[index, sup] = summed.astype(jnp.bfloat16)

        @pl.when(index < chunks - 1)
        def _():
            for step in range(1, row_count):
                send_p(index, step).start()

        return carry

    lax.fori_loop(0, chunks, work, 0)

    for sup in range(row_count):
        quad_send[sup] = (quad[sup, :, :TILE] + quad[sup, :, TILE:]).astype(jnp.bfloat16)
    for step in range(1, row_count):
        send_q(step).start()
    for step in range(1, row_count):
        send_p(chunks - 1, step).start()
    once = jnp.where(row == 0, 1.0, 0.0)
    share = quad[high, :, :TILE] + quad[high, :, TILE:]
    for pole in range(poles):
        share = share + (once * weight_ref[pole, 0]) * diag_ref[pole, 0, 0]
        share = share - (once * weight_ref[pole, 1]) * diag_ref[pole, 1, 0]
    for step in range(1, row_count):
        send_q(step).wait_recv()
        share = share + quad_recv[step - 1].astype(jnp.float32)
    shares[row, core] = share
    for which in reversed(range(len(others))):
        send_s(which).start()
    for index in range(chunks):
        finish(index)
    for index in range(chunks):
        send_c(index).wait_recv()
        panel_out[index * chunk : (index + 1) * chunk, :] = final[index] + final_recv[index]
    for which in range(len(others)):
        send_s(which).wait_recv()
    value = shares[0, 0]
    for at in range(1, 2 * row_count):
        value = value + shares[at // 2, at % 2]
    diag_out[0] = value

    for at in range(pieces):
        for step in range(1, row_count):
            send_m(at, step).wait_send()

    @pl.when(row == high)
    def _():
        for at in range(pieces):
            for step in range(row_count):
                for across in range(1, row_count):
                    send_x(at, step, across).wait_send()

    for index in range(chunks):
        send_g(index).wait_send()
        send_c(index).wait_send()
        for step in range(1, row_count):
            send_p(index, step).wait_send()
    for step in range(1, row_count):
        send_q(step).wait_send()
    for which in range(len(others)):
        send_s(which).wait_send()


def shards(row_count, inverse_block, lower_panel, tile_pattern, diag_inverse, pole_weight):
    poles, _, rows, half = inverse_block.shape
    chunk = 256
    chunks = rows // chunk
    vmem = pl.BlockSpec(memory_space=pltpu.VMEM)
    hbm = pl.BlockSpec(memory_space=pltpu.HBM)
    dma = pltpu.SemaphoreType.DMA
    bf16, f32 = jnp.bfloat16, jnp.float32
    steps = row_count - 1
    flops = 2 * poles * rows * half * 2 * TILE * row_count * 5
    return pl.pallas_call(
        functools.partial(kernel, row_count, chunk),
        out_shape=(
            jax.ShapeDtypeStruct((rows, TILE), f32),
            jax.ShapeDtypeStruct((1, TILE, TILE), f32),
        ),
        in_specs=[hbm] * 5,
        out_specs=(vmem, vmem),
        scratch_shapes=[
            pltpu.SMEM(tile_pattern.shape, jnp.int32),
            pltpu.SMEM(pole_weight.shape, f32),
            pltpu.VMEM(inverse_block.shape, bf16),
            pltpu.VMEM(lower_panel.shape, bf16),
            pltpu.VMEM(diag_inverse.shape, f32),
            dma((5,)),
            pltpu.VMEM((poles, row_count, 2, rows, 2 * TILE), f32),
            pltpu.VMEM((2, row_count, poles, 2, rows, TILE), bf16),
            pltpu.VMEM((poles, 2, rows, half), bf16),
            pltpu.VMEM((row_count, rows, TILE), f32),
            pltpu.VMEM((chunks, row_count, chunk, TILE), bf16),
            pltpu.VMEM((chunks, steps, chunk, TILE), bf16),
            pltpu.VMEM((chunks, chunk, TILE), f32),
            pltpu.VMEM((chunks, chunk, TILE), f32),
            pltpu.VMEM((row_count, TILE, 2 * TILE), f32),
            pltpu.VMEM((row_count, TILE, TILE), bf16),
            pltpu.VMEM((steps, TILE, TILE), bf16),
            pltpu.VMEM((row_count, 2, TILE, TILE), f32),
            dma((steps, 2 * poles)),
            dma((steps, 2 * poles)),
            dma((steps, row_count, 2 * poles)),
            dma((row_count, 2 * poles)),
            dma((chunks,)),
            dma((chunks,)),
            dma((chunks, steps)),
            dma((chunks, steps)),
            dma((chunks,)),
            dma((chunks,)),
            dma((steps,)),
            dma((steps,)),
            dma((2 * row_count - 1,)),
            dma((2 * row_count - 1,)),
        ],
        compiler_params=pltpu.CompilerParams(
            collective_id=0, has_side_effects=True, vmem_limit_bytes=62 * 1024 * 1024
        ),
        cost_estimate=pl.CostEstimate(flops=flops, bytes_accessed=4 * 1024 * 1024, transcendentals=0),
    )(tile_pattern, pole_weight, inverse_block, lower_panel, diag_inverse)


def solution(mesh):
    placed = (
        P(("groups", "pole"), None, "grow", "gcol"),
        P(("groups", "pole"), None, "grow", "gcol"),
        P("groups", None),
        P(("groups", "pole"), None, "gcol", None, None),
        P(("groups", "pole"), None),
    )
    return jax.shard_map(
        functools.partial(shards, mesh.shape["grow"]),
        mesh=mesh,
        in_specs=placed,
        out_specs=(P(("groups", "grow"), "gcol"), P(("groups", "gcol"), None, None)),
        check_vma=False,
    )
```

```python
import functools

import jax
import jax.numpy as jnp
from jax import lax
from jax.experimental import pallas as pl
from jax.experimental.pallas import tpu as pltpu
from jax.sharding import PartitionSpec as P

TILE = 128
MESH = pl.DeviceIdType.MESH


def kernel(
    row_count,
    chunk,
    pattern_hbm,
    weight_hbm,
    inverse_hbm,
    lower_hbm,
    diag_hbm,
    panel_out,
    diag_out,
    pattern_ref,
    weight_ref,
    inverse_ref,
    lower_ref,
    diag_ref,
    load_sem,
    early,
    panels,
    inverse_next,
    total,
    panel_send,
    panel_recv,
    final,
    final_recv,
    quad,
    quad_send,
    quad_recv,
    shares,
    m_send,
    m_recv,
    x_send,
    x_recv,
    g_send,
    g_recv,
    p_send,
    p_recv,
    c_send,
    c_recv,
    q_send,
    q_recv,
    s_send,
    s_recv,
):
    poles, _, rows, half = inverse_ref.shape
    chunks = rows // chunk
    row_tiles = rows // TILE
    row = lax.axis_index("grow")
    col = lax.axis_index("gcol")
    core = lax.axis_index("pole")
    high, low = col // 2, col % 2
    inner = jnp.where(row == high, 0, 1)

    def to_high(step):
        return {"gcol": lax.rem(high + step, row_count) * 2 + low}

    def to_row(step):
        return {"grow": lax.rem(row + step, row_count)}

    def piece(at):
        return at, pl.ds(0, rows)

    pieces = poles

    def send_m(at, step):
        pole, part = piece(at)
        return pltpu.make_async_remote_copy(
            src_ref=panels.at[0, high, pole, :, part],
            dst_ref=panels.at[0, high, pole, :, part],
            send_sem=m_send.at[step - 1, at],
            recv_sem=m_recv.at[step - 1, at],
            device_id=to_high(step),
            device_id_type=MESH,
        )

    def send_x(at, step, across):
        pole, part = piece(at)
        sup = lax.rem(high + row_count - step, row_count)
        return pltpu.make_async_remote_copy(
            src_ref=panels.at[0, sup, pole, :, part],
            dst_ref=panels.at[1, sup, pole, :, part],
            send_sem=x_send.at[across - 1, step, at],
            recv_sem=x_recv.at[step, at],
            device_id=to_row(across),
            device_id_type=MESH,
        )

    def send_g(index):
        cut = pl.ds(pl.multiple_of(index * chunk, chunk), chunk)
        return pltpu.make_async_remote_copy(
            src_ref=inverse_hbm.at[:, :, cut, :],
            dst_ref=inverse_next.at[:, :, cut, :],
            send_sem=g_send.at[index],
            recv_sem=g_recv.at[index],
            device_id={"gcol": high * 2 + 1 - low},
            device_id_type=MESH,
        )

    def send_p(index, step):
        return pltpu.make_async_remote_copy(
            src_ref=panel_send.at[index, lax.rem(high + step, row_count)],
            dst_ref=panel_recv.at[index, step - 1],
            send_sem=p_send.at[index, step - 1],
            recv_sem=p_recv.at[index, step - 1],
            device_id=to_high(step),
            device_id_type=MESH,
        )

    def send_c(index):
        return pltpu.make_async_remote_copy(
            src_ref=final.at[index],
            dst_ref=final_recv.at[index],
            send_sem=c_send.at[index],
            recv_sem=c_recv.at[index],
            device_id={"pole": 1 - core},
            device_id_type=MESH,
        )

    def send_q(step):
        return pltpu.make_async_remote_copy(
            src_ref=quad_send.at[lax.rem(high + step, row_count)],
            dst_ref=quad_recv.at[step - 1],
            send_sem=q_send.at[step - 1],
            recv_sem=q_recv.at[step - 1],
            device_id=to_high(step),
            device_id_type=MESH,
        )

    others = [(across, flip) for across in range(row_count) for flip in range(2) if (across, flip) != (0, 0)]

    def send_s(which):
        across, flip = others[which]
        return pltpu.make_async_remote_copy(
            src_ref=shares.at[row, core],
            dst_ref=shares.at[row, core],
            send_sem=s_send.at[which],
            recv_sem=s_recv.at[which],
            device_id={"grow": lax.rem(row + across, row_count), "pole": lax.rem(core + flip, 2)},
            device_id_type=MESH,
        )

    barrier = pltpu.get_barrier_semaphore()
    peers = [{"gcol": high * 2 + 1 - low}]
    peers += [to_high(step) for step in range(1, row_count)]
    peers += [
        {"grow": lax.rem(row + across, row_count), "pole": lax.rem(core + flip, 2)} for across, flip in others
    ]
    for peer in peers:
        pl.semaphore_signal(barrier, inc=1, device_id=peer, device_id_type=MESH)

    loads = [
        pltpu.make_async_copy(source, target, load_sem.at[at])
        for at, (source, target) in enumerate(
            (
                (pattern_hbm, pattern_ref),
                (lower_hbm, lower_ref),
                (weight_hbm, weight_ref),
                (inverse_hbm, inverse_ref),
                (diag_hbm, diag_ref),
            )
        )
    ]
    for load in loads:
        load.start()
    loads[0].wait()
    loads[1].wait()

    for tile in range(row_tiles):
        present = pattern_ref[col, row * row_tiles + tile].astype(jnp.float32).astype(jnp.bfloat16)
        cut = slice(tile * TILE, (tile + 1) * TILE)
        for pole in range(poles):
            panels[0, high, pole, :, cut, :] = lower_ref[pole, :, cut, :] * present

    pl.semaphore_wait(barrier, len(peers))

    for at in range(pieces):
        for step in range(1, row_count):
            send_m(at, step).start()

    @pl.when(row == high)
    def _():
        for at in range(pieces):
            for across in range(1, row_count):
                send_x(at, 0, across).start()

    ahead = 1
    for index in range(ahead):
        send_g(index).start()

    quad[...] = jnp.zeros_like(quad)
    for load in loads[2:]:
        load.wait()

    for at in range(pieces):
        for step in range(1, row_count):
            send_m(at, step).wait_recv()
            if step == 1:
                for index in ((1,), (), (), ())[at]:
                    send_g(index).start()

            @pl.when(row == high)
            def _():
                for across in range(1, row_count):
                    send_x(at, step, across).start()

    @pl.when(row != high)
    def _():
        for at in range(pieces):
            for step in range(row_count):
                send_x(at, step, 1).wait_recv()

    def finish(index):
        cut = pl.ds(pl.multiple_of(index * chunk, chunk), chunk)
        value = total[high, cut, :]
        for step in range(1, row_count):
            send_p(index, step).wait_recv()
            value = value + panel_recv[index, step - 1].astype(jnp.float32)
        final[index] = value
        send_c(index).start()

    own_rows = pl.ds(pl.multiple_of(low * half, half), half)
    next_rows = pl.ds(pl.multiple_of((1 - low) * half, half), half)

    def dot(left, right):
        return jnp.dot(left, right, preferred_element_type=jnp.float32)

    def begin(index, carry):
        cut = pl.ds(pl.multiple_of(index * chunk, chunk), chunk)
        for sup in range(row_count):
            for pole in range(poles):
                m_own = jnp.concatenate(
                    [panels[inner, sup, pole, 0, own_rows, :], panels[inner, sup, pole, 1, own_rows, :]], axis=1
                )
                for part in range(2):
                    early[pole, sup, part, cut, :] = dot(inverse_ref[pole, part, cut, :], m_own)
        return carry

    lax.fori_loop(0, chunks, begin, 0)

    def work(index, carry):
        cut = pl.ds(pl.multiple_of(index * chunk, chunk), chunk)
        send_g(index).wait_recv()
        for sup in range(row_count):
            summed = None
            for pole in range(poles):
                m_next = jnp.concatenate(
                    [panels[inner, sup, pole, 0, next_rows, :], panels[inner, sup, pole, 1, next_rows, :]], axis=1
                )
                by_re = early[pole, sup, 0, cut, :] + dot(inverse_next[pole, 0, cut, :], m_next)
                by_im = early[pole, sup, 1, cut, :] + dot(inverse_next[pole, 1, cut, :], m_next)
                solved_re = by_im[:, TILE:] - by_re[:, :TILE]
                solved_im = -(by_re[:, TILE:] + by_im[:, :TILE])
                w_re, w_im = weight_ref[pole, 0], weight_ref[pole, 1]
                scaled_re = w_re * solved_re - w_im * solved_im
                scaled_im = w_re * solved_im + w_im * solved_re
                summed = scaled_re if summed is None else summed + scaled_re
                stacked = jnp.concatenate([-scaled_re, scaled_im], axis=0)
                upper = stacked.astype(jnp.bfloat16)
                rest = (stacked - upper.astype(jnp.float32)).astype(jnp.bfloat16)
                m_rows = jnp.concatenate(
                    [panels[0, sup, pole, 0, cut, :], panels[0, sup, pole, 1, cut, :]], axis=0
                )
                quad[sup] += lax.dot_general(
                    m_rows,
                    jnp.concatenate([upper, rest], axis=1),
                    (((0,), (0,)), ((), ())),
                    preferred_element_type=jnp.float32,
                )
            total[sup, cut, :] = summed
            panel_send[index, sup] = summed.astype(jnp.bfloat16)

        @pl.when(index < chunks - 1)
        def _():
            for step in range(1, row_count):
                send_p(index, step).start()

        return carry

    lax.fori_loop(0, chunks, work, 0)

    for sup in range(row_count):
        quad_send[sup] = (quad[sup, :, :TILE] + quad[sup, :, TILE:]).astype(jnp.bfloat16)
    for step in range(1, row_count):
        send_q(step).start()
    for step in range(1, row_count):
        send_p(chunks - 1, step).start()
    once = jnp.where(row == 0, 1.0, 0.0)
    share = quad[high, :, :TILE] + quad[high, :, TILE:]
    for pole in range(poles):
        share = share + (once * weight_ref[pole, 0]) * diag_ref[pole, 0, 0]
        share = share - (once * weight_ref[pole, 1]) * diag_ref[pole, 1, 0]
    for step in range(1, row_count):
        send_q(step).wait_recv()
        share = share + quad_recv[step - 1].astype(jnp.float32)
    shares[row, core] = share
    for which in reversed(range(len(others))):
        send_s(which).start()
    for index in range(chunks):
        finish(index)
    for index in range(chunks):
        send_c(index).wait_recv()
        panel_out[index * chunk : (index + 1) * chunk, :] = final[index] + final_recv[index]
    for which in range(len(others)):
        send_s(which).wait_recv()
    value = shares[0, 0]
    for at in range(1, 2 * row_count):
        value = value + shares[at // 2, at % 2]
    diag_out[0] = value

    for at in range(pieces):
        for step in range(1, row_count):
            send_m(at, step).wait_send()

    @pl.when(row == high)
    def _():
        for at in range(pieces):
            for step in range(row_count):
                for across in range(1, row_count):
                    send_x(at, step, across).wait_send()

    for index in range(chunks):
        send_g(index).wait_send()
        send_c(index).wait_send()
        for step in range(1, row_count):
            send_p(index, step).wait_send()
    for step in range(1, row_count):
        send_q(step).wait_send()
    for which in range(len(others)):
        send_s(which).wait_send()


def shards(row_count, inverse_block, lower_panel, tile_pattern, diag_inverse, pole_weight):
    poles, _, rows, half = inverse_block.shape
    chunk = 256
    chunks = rows // chunk
    vmem = pl.BlockSpec(memory_space=pltpu.VMEM)
    hbm = pl.BlockSpec(memory_space=pltpu.HBM)
    dma = pltpu.SemaphoreType.DMA
    bf16, f32 = jnp.bfloat16, jnp.float32
    steps = row_count - 1
    flops = 2 * poles * rows * half * 2 * TILE * row_count * 5
    return pl.pallas_call(
        functools.partial(kernel, row_count, chunk),
        out_shape=(
            jax.ShapeDtypeStruct((rows, TILE), f32),
            jax.ShapeDtypeStruct((1, TILE, TILE), f32),
        ),
        in_specs=[hbm] * 5,
        out_specs=(vmem, vmem),
        scratch_shapes=[
            pltpu.SMEM(tile_pattern.shape, jnp.int32),
            pltpu.SMEM(pole_weight.shape, f32),
            pltpu.VMEM(inverse_block.shape, bf16),
            pltpu.VMEM(lower_panel.shape, bf16),
            pltpu.VMEM(diag_inverse.shape, f32),
            dma((5,)),
            pltpu.VMEM((poles, row_count, 2, rows, 2 * TILE), f32),
            pltpu.VMEM((2, row_count, poles, 2, rows, TILE), bf16),
            pltpu.VMEM((poles, 2, rows, half), bf16),
            pltpu.VMEM((row_count, rows, TILE), f32),
            pltpu.VMEM((chunks, row_count, chunk, TILE), bf16),
            pltpu.VMEM((chunks, steps, chunk, TILE), bf16),
            pltpu.VMEM((chunks, chunk, TILE), f32),
            pltpu.VMEM((chunks, chunk, TILE), f32),
            pltpu.VMEM((row_count, TILE, 2 * TILE), f32),
            pltpu.VMEM((row_count, TILE, TILE), bf16),
            pltpu.VMEM((steps, TILE, TILE), bf16),
            pltpu.VMEM((row_count, 2, TILE, TILE), f32),
            dma((steps, 2 * poles)),
            dma((steps, 2 * poles)),
            dma((steps, row_count, 2 * poles)),
            dma((row_count, 2 * poles)),
            dma((chunks,)),
            dma((chunks,)),
            dma((chunks, steps)),
            dma((chunks, steps)),
            dma((chunks,)),
            dma((chunks,)),
            dma((steps,)),
            dma((steps,)),
            dma((2 * row_count - 1,)),
            dma((2 * row_count - 1,)),
        ],
        compiler_params=pltpu.CompilerParams(
            collective_id=0, has_side_effects=True, vmem_limit_bytes=62 * 1024 * 1024
        ),
        cost_estimate=pl.CostEstimate(flops=flops, bytes_accessed=4 * 1024 * 1024, transcendentals=0),
    )(tile_pattern, pole_weight, inverse_block, lower_panel, diag_inverse)


def solution(mesh):
    placed = (
        P(("groups", "pole"), None, "grow", "gcol"),
        P(("groups", "pole"), None, "grow", "gcol"),
        P("groups", None),
        P(("groups", "pole"), None, "gcol", None, None),
        P(("groups", "pole"), None),
    )
    return jax.shard_map(
        functools.partial(shards, mesh.shape["grow"]),
        mesh=mesh,
        in_specs=placed,
        out_specs=(P(("groups", "grow"), "gcol"), P(("groups", "gcol"), None, None)),
        check_vma=False,
    )
```
